768 devices in a mesh: dp: 192 (over y, z_lo, x, core), fsdp: 4 (over z_hi).
Axes of the slice: x: 4, y: 8, z: 12 (z_hi: 4, z_lo: 3; z = z_hi * 3 + z_lo), core: 2. Of those that a mesh axis runs over, the one named last changes fastest.
Arguments:
- queries: bfloat16 [98304, 2048], P(('dp', 'fsdp')), may hold values from -100 to 100
- keys: bfloat16 [98304, 2048], P(('dp', 'fsdp')), may hold values from -4 to 4
- values: bfloat16 [98304, 2048], P(('dp', 'fsdp')), may hold values from -6 to 6
- doc_mask: int32 [98304, 384], P(('dp', 'fsdp')), may hold values from 0 to 1, as said below
- ratio_bins: int32 [98304], P(('dp', 'fsdp')), may hold values from 0 to 7
- out_grad: bfloat16 [98304, 2048], P(('dp', 'fsdp')), may hold values from -6 to 6
Outputs:
- attended: bfloat16 [98304, 2048], P(('dp', 'fsdp'))
- query_grad: bfloat16 [98304, 2048], P(('dp', 'fsdp'))
- key_grad: bfloat16 [98304, 2048], P(('dp', 'fsdp'))
- value_grad: bfloat16 [98304, 2048], P(('dp', 'fsdp'))
The draws below stay inside these ranges and needn't reach their ends.
Inputs may be any that keep to these rules, and one draw needn't show every extreme that they name: `doc_mask`: entry (i, c) is 1 exactly where key position g = (i // 128) * 128 - 128 + c exists and lies in the same packed document as token i; every token marks itself, and no document spans more than two neighbouring devices.
All inputs are finite; a program needn't handle non-finite values.
Results may differ from the reference program's by a relative error of at most 0.04.
Values may be sent and summed in bfloat16 or wider, within the bound.
A program may use at most 64 MiB of HBM per device.

```python
import math
import jax
import jax.numpy as jnp
from jax import lax

TOK_DEV = 128
HEADS = 16
HEAD_DIM = 128
NBINS = 8
TOKENS = 98304


def shared_base(key):
    return jnp.clip(jax.random.normal(key, (TOKENS, HEADS * HEAD_DIM), jnp.float32), -4.0, 4.0)


def draw_keys(key, part):
    base = shared_base(key)
    return base.astype(jnp.bfloat16)


def draw_queries(key, part):
    key = jax.random.fold_in(key, 5)
    fresh = jnp.clip(jax.random.normal(key, (TOKENS, HEADS * HEAD_DIM), jnp.float32), -4.0, 4.0)
    return fresh.astype(jnp.bfloat16)


def draw_doc_mask(key, part):
    key = jax.random.fold_in(key, 11)
    blocks = TOKENS // TOK_DEV
    extra = (jax.random.randint(jax.random.fold_in(key, 1), (TOKENS,), 0, 64) == 0).astype(jnp.int32)
    offsets = jax.random.randint(jax.random.fold_in(key, 2), (blocks,), 0, TOK_DEV)
    forced = (jnp.arange(TOK_DEV)[None, :] == offsets[:, None]).astype(jnp.int32).reshape(TOKENS)
    starts = jnp.maximum(extra, forced)
    doc_ids = jnp.cumsum(starts).astype(jnp.int32).reshape(blocks, TOK_DEV)
    outside = jnp.full((1, TOK_DEV), -1, jnp.int32)
    left_ids = jnp.concatenate([outside, doc_ids[:-1]], axis=0)
    right_ids = jnp.concatenate([doc_ids[1:], outside], axis=0)
    window = jnp.concatenate([left_ids, doc_ids, right_ids], axis=1)
    same_doc = doc_ids[:, :, None] == window[:, None, :]
    return same_doc.astype(jnp.int32).reshape(TOKENS, 3 * TOK_DEV)


def plant(entries, own_key, low, high):
    shape = entries.shape
    spot = [jax.random.randint(jax.random.fold_in(own_key, axis), (), 0, shape[axis]) for axis in range(len(shape))]
    entries = entries.at[tuple(spot)].set(low)
    longest = shape.index(max(shape))
    spot[longest] = (spot[longest] + 1) % shape[longest]
    return entries.at[tuple(spot)].set(high)


def block_scale(stream_key, shape, shards, low, high):
    factor_of = 1.0
    for axis_at, parts in shards:
        steps = jax.random.uniform(jax.random.fold_in(jax.random.fold_in(stream_key, 6), axis_at), (parts,), jnp.float32, low / len(shards), high / len(shards))
        factor_of = factor_of * jnp.repeat(jnp.exp(steps), shape[axis_at] // parts).reshape((-1,) + (1,) * (len(shape) - 1 - axis_at))
    return factor_of


def scatter_about(rng, dims, spread, most, cuts=(), held_as=jnp.bfloat16):
    values = jax.random.normal(rng, dims, jnp.float32) * spread
    if len(cuts) > 0:
        values = block_scale(rng, dims, cuts, -0.22, 0.18) * values
    return jnp.clip(values, min=-most, max=most).astype(held_as)


def setup_inputs(seed: int = 0) -> dict:
    seeds = jax.random.split(jax.random.key(seed), 7)
    return {
        "queries": draw_queries(jax.random.fold_in(seeds[6], 71), 0),
        "keys": draw_keys(jax.random.fold_in(seeds[6], 71), 0),
        "values": scatter_about(seeds[2], (TOKENS, HEADS * HEAD_DIM), 1.0, 6.0, ((0, 768),)),
        "doc_mask": draw_doc_mask(jax.random.fold_in(seeds[6], 71), 0),
        "ratio_bins": plant(jax.random.randint(seeds[4], (TOKENS,), 0, NBINS), jax.random.fold_in(seeds[4], 1), 0, NBINS - 1).astype(jnp.int32),
        "out_grad": scatter_about(seeds[5], (TOKENS, HEADS * HEAD_DIM), 1.0, 6.0, ((0, 768),)),
    }


masked_score = -1e+30

def split_heads(matrix):
    return matrix.reshape(matrix.shape[0], HEADS, HEAD_DIM)

def forward_block(query_rows, key_window, value_window, allowed, scaled_rows):
    score_scale = 1.0 / math.sqrt(HEAD_DIM)
    query_f = split_heads(query_rows).astype(jnp.float32)
    key_f = split_heads(key_window).astype(jnp.float32)
    value_f = split_heads(value_window).astype(jnp.float32)
    grad_f = split_heads(scaled_rows).astype(jnp.float32)
    scores = jnp.einsum('ihd,jhd->hij', query_f, key_f) * score_scale
    scores = jnp.where(allowed[None], scores, masked_score)
    largest = lax.optimization_barrier(jnp.max(scores, axis=2, keepdims=True))
    log_total = largest + jnp.log(lax.optimization_barrier(jnp.sum(jnp.exp(scores - largest), axis=2, keepdims=True)))
    softmax_w = jnp.exp(scores - log_total)
    rounded_w = lax.optimization_barrier(softmax_w.astype(jnp.bfloat16)).astype(jnp.float32)
    attended = jnp.einsum('hij,jhd->ihd', rounded_w, value_f).reshape(query_rows.shape).astype(jnp.bfloat16)
    delta = jnp.transpose(lax.optimization_barrier(jnp.sum(grad_f * split_heads(attended).astype(jnp.float32), axis=2)))
    dprob = jnp.einsum('ihd,jhd->hij', grad_f, value_f)
    dscore = softmax_w * (dprob - delta[:, :, None])
    dscore = lax.optimization_barrier(dscore.astype(jnp.bfloat16)).astype(jnp.float32)
    query_grad = (jnp.einsum('hij,jhd->ihd', dscore, key_f) * score_scale).reshape(query_rows.shape).astype(jnp.bfloat16)
    return (attended, query_grad, log_total[:, :, 0], delta)

def key_block(query_rows, scaled_rows, key_rows, value_rows, allowed, log_total, delta):
    score_scale = 1.0 / math.sqrt(HEAD_DIM)
    query_f = split_heads(query_rows).astype(jnp.float32)
    key_f = split_heads(key_rows).astype(jnp.float32)
    value_f = split_heads(value_rows).astype(jnp.float32)
    grad_f = split_heads(scaled_rows).astype(jnp.float32)
    scores = jnp.einsum('ihd,jhd->hij', query_f, key_f) * score_scale
    scores = jnp.where(allowed[None], scores, masked_score)
    softmax_w = jnp.exp(scores - log_total[:, :, None])
    rounded_w = lax.optimization_barrier(softmax_w.astype(jnp.bfloat16)).astype(jnp.float32)
    dprob = jnp.einsum('ihd,jhd->hij', grad_f, value_f)
    dscore = softmax_w * (dprob - delta[:, :, None])
    dscore = lax.optimization_barrier(dscore.astype(jnp.bfloat16)).astype(jnp.float32)
    key_grad = (jnp.einsum('hij,ihd->jhd', dscore, query_f) * score_scale).reshape(key_rows.shape).astype(jnp.bfloat16)
    value_grad = jnp.einsum('hij,ihd->jhd', rounded_w, grad_f).reshape(key_rows.shape).astype(jnp.bfloat16)
    return (key_grad, value_grad)

def reference(queries, keys, values, doc_mask, ratio_bins, out_grad):
    blocks = TOKENS // TOK_DEV
    width = HEADS * HEAD_DIM
    weight = NBINS / (ratio_bins.astype(jnp.float32) + 1.0)
    scaled = (out_grad.astype(jnp.float32) * weight[:, None]).astype(jnp.bfloat16)
    padding = jnp.zeros((TOK_DEV, width), jnp.bfloat16)
    key_pad = jnp.concatenate([padding, keys, padding], axis=0)
    value_pad = jnp.concatenate([padding, values, padding], axis=0)
    query_pad = jnp.concatenate([padding, queries, padding], axis=0)
    scaled_pad = jnp.concatenate([padding, scaled, padding], axis=0)
    mask_padding = jnp.zeros((TOK_DEV, 3 * TOK_DEV), jnp.int32)
    mask_pad = jnp.concatenate([mask_padding, doc_mask, mask_padding], axis=0)

    def forward_step(index):
        start = (index * TOK_DEV).astype(jnp.int32)
        query_rows = lax.dynamic_slice_in_dim(queries, start, TOK_DEV, 0)
        key_window = lax.dynamic_slice_in_dim(key_pad, start, 3 * TOK_DEV, 0)
        value_window = lax.dynamic_slice_in_dim(value_pad, start, 3 * TOK_DEV, 0)
        allowed = lax.dynamic_slice_in_dim(doc_mask, start, TOK_DEV, 0) == 1
        scaled_rows = lax.dynamic_slice_in_dim(scaled, start, TOK_DEV, 0)
        return forward_block(query_rows, key_window, value_window, allowed, scaled_rows)
    emitted = lax.map(forward_step, jnp.arange(blocks, dtype=jnp.int32))
    attended = emitted[0].reshape(TOKENS, width)
    query_grad = emitted[1].reshape(TOKENS, width)
    stat_padding = jnp.zeros((HEADS, TOK_DEV), jnp.float32)
    total_all = jnp.transpose(emitted[2], (1, 0, 2)).reshape(HEADS, TOKENS)
    delta_all = jnp.transpose(emitted[3], (1, 0, 2)).reshape(HEADS, TOKENS)
    total_pad = jnp.concatenate([stat_padding, total_all, stat_padding], axis=1)
    delta_pad = jnp.concatenate([stat_padding, delta_all, stat_padding], axis=1)

    def gradient_step(index):
        start = (index * TOK_DEV).astype(jnp.int32)
        query_rows = lax.dynamic_slice_in_dim(query_pad, start, 3 * TOK_DEV, 0)
        scaled_rows = lax.dynamic_slice_in_dim(scaled_pad, start, 3 * TOK_DEV, 0)
        key_rows = lax.dynamic_slice_in_dim(keys, start, TOK_DEV, 0)
        value_rows = lax.dynamic_slice_in_dim(values, start, TOK_DEV, 0)
        mask_rows = lax.dynamic_slice_in_dim(mask_pad, start, 3 * TOK_DEV, 0)
        allowed = jnp.concatenate([mask_rows[:TOK_DEV, 2 * TOK_DEV:], mask_rows[TOK_DEV:2 * TOK_DEV, TOK_DEV:2 * TOK_DEV], mask_rows[2 * TOK_DEV:, :TOK_DEV]], axis=0) == 1
        log_total = lax.dynamic_slice_in_dim(total_pad, start, 3 * TOK_DEV, 1)
        delta = lax.dynamic_slice_in_dim(delta_pad, start, 3 * TOK_DEV, 1)
        return key_block(query_rows, scaled_rows, key_rows, value_rows, allowed, log_total, delta)
    grads = lax.map(gradient_step, jnp.arange(blocks, dtype=jnp.int32))
    key_grad = grads[0].reshape(TOKENS, width)
    value_grad = grads[1].reshape(TOKENS, width)
    return (attended, query_grad, key_grad, value_grad)
```

```python
import functools
import math

import jax
import jax.numpy as jnp
from jax import lax
from jax.experimental import pallas as pl
from jax.experimental.pallas import tpu as pltpu
from jax.sharding import PartitionSpec as P

HEADS = 16
HEAD_DIM = 128
NBINS = 8
GROUP = 2
GROUPS = HEADS // GROUP
COLS = GROUP * HEAD_DIM
MASKED = -1e30
MESH = pl.DeviceIdType.MESH


def neighbour(step):
    dps, fsdps = lax.axis_size("dp"), lax.axis_size("fsdp")
    flat = lax.axis_index("dp") * fsdps + lax.axis_index("fsdp")
    flat = lax.rem(flat + step + dps * fsdps, dps * fsdps)
    return (flat // fsdps, lax.rem(flat, fsdps))


def dot(a, b, dims):
    return lax.dot_general(a, b, (dims, ((), ())), preferred_element_type=jnp.float32)


def kernel(
    queries, keys, values, out_grad, mask, bins,
    attended, query_grad, key_grad, value_grad,
    q_v, k_v, v_v, g_v, halo, sent, got, own, bias, weight,
    load_sem, halo_send, halo_recv, term_send, term_recv,
):
    scale = 1.0 / math.sqrt(HEAD_DIM)
    rows = q_v.shape[0]
    sides = (neighbour(-1), neighbour(1))

    def load(at, src, dst):
        return pltpu.make_async_copy(src, dst, load_sem.at[at])

    loads = [
        load(0, queries, q_v), load(1, keys, k_v), load(2, values, v_v), load(3, out_grad, g_v)
    ]
    for copy in loads:
        copy.start()

    barrier = pltpu.get_barrier_semaphore()
    for side in sides:
        pl.semaphore_signal(barrier, inc=1, device_id=side, device_id_type=MESH)
    pl.semaphore_wait(barrier, 2)

    def columns(group):
        return pl.ds(pl.multiple_of(group * COLS, COLS), COLS)

    def halo_copy(group, kind, side):
        src = (keys, values)[kind]
        at = (kind * 2 + 1 - side) * GROUPS + group
        return pltpu.make_async_remote_copy(
            src_ref=src.at[:, columns(group)],
            dst_ref=halo.at[kind, 1 - side, :, columns(group)],
            send_sem=halo_send.at[at],
            recv_sem=halo_recv.at[at],
            device_id=sides[side],
            device_id_type=MESH,
        )

    def term_copy(group, kind, side):
        at = (kind * 2 + 1 - side) * GROUPS + group
        return pltpu.make_async_remote_copy(
            src_ref=sent.at[kind, side, :, columns(group)],
            dst_ref=got.at[kind, 1 - side, :, columns(group)],
            send_sem=term_send.at[at],
            recv_sem=term_recv.at[at],
            device_id=sides[side],
            device_id_type=MESH,
        )

    each = [(kind, side) for kind in range(2) for side in range(2)]

    def send_halo(group, carry):
        for kind, side in each:
            halo_copy(group, kind, side).start()
        return carry

    lax.fori_loop(0, GROUPS, send_halo, 0)

    bias[...] = jnp.where(mask[...] == 1, 0.0, MASKED)
    ratio = NBINS / (bins[...].astype(jnp.float32) + 1.0)
    weight[...] = jnp.broadcast_to(ratio, (HEAD_DIM, rows)).T
    for copy in loads:
        copy.wait()

    def attend(group, carry):
        for kind, side in each:
            halo_copy(group, kind, side).wait_recv()
        for head in range(GROUP):
            here = pl.ds(
                pl.multiple_of(group * COLS + head * HEAD_DIM, HEAD_DIM), HEAD_DIM
            )
            q = q_v[:, here]
            g = (g_v[:, here].astype(jnp.float32) * weight[...]).astype(jnp.bfloat16)
            k = jnp.concatenate([halo[0, 0, :, here], k_v[:, here], halo[0, 1, :, here]], axis=0)
            v = jnp.concatenate([halo[1, 0, :, here], v_v[:, here], halo[1, 1, :, here]], axis=0)
            allowed = bias[...] == 0.0
            scores = jnp.where(allowed, dot(q, k, ((1,), (1,))) * scale, MASKED)
            largest = jnp.max(scores, axis=1, keepdims=True)
            powers = jnp.exp(scores - largest)
            prob = powers / jnp.sum(powers, axis=1, keepdims=True)
            prob_w = prob.astype(jnp.bfloat16)
            out = dot(prob_w, v, ((1,), (0,))).astype(jnp.bfloat16)
            attended[:, here] = out
            delta = jnp.sum(
                g.astype(jnp.float32) * out.astype(jnp.float32), axis=1, keepdims=True
            )
            dprob = dot(g, v, ((1,), (1,)))
            dscore = (prob * (dprob - delta)).astype(jnp.bfloat16)
            query_grad[:, here] = (dot(dscore, k, ((1,), (0,))) * scale).astype(jnp.bfloat16)
            dk = dot(dscore, q, ((0,), (0,))) * scale
            dv = dot(prob_w, g, ((0,), (0,)))
            for kind, term in ((0, dk), (1, dv)):
                sent[kind, 0, :, here] = term[:rows].astype(jnp.bfloat16)
                own[kind, :, here] = term[rows : 2 * rows]
                sent[kind, 1, :, here] = term[2 * rows :].astype(jnp.bfloat16)
        for kind, side in each:
            term_copy(group, kind, side).start()
        return carry

    lax.fori_loop(0, GROUPS, attend, 0)

    def finish(group, carry):
        for kind, side in each:
            term_copy(group, kind, side).wait_recv()
        for kind, grad in ((0, key_grad), (1, value_grad)):
            here = columns(group)
            total = own[kind, :, here] + got[kind, 0, :, here].astype(jnp.float32)
            grad[:, here] = (total + got[kind, 1, :, here].astype(jnp.float32)).astype(jnp.bfloat16)
        return carry

    lax.fori_loop(0, GROUPS, finish, 0)

    def drain(group, carry):
        for kind, side in each:
            halo_copy(group, kind, side).wait_send()
            term_copy(group, kind, side).wait_send()
        return carry

    lax.fori_loop(0, GROUPS, drain, 0)


def local(queries, keys, values, doc_mask, ratio_bins, out_grad):
    rows, width = queries.shape
    result = jax.ShapeDtypeStruct((rows, width), jnp.bfloat16)
    any_space = pl.BlockSpec(memory_space=pl.ANY)
    vmem = pl.BlockSpec(memory_space=pltpu.VMEM)
    block = pltpu.VMEM((rows, width), jnp.bfloat16)
    return pl.pallas_call(
        kernel,
        out_shape=[result] * 4,
        in_specs=[any_space] * 4 + [vmem] * 2,
        out_specs=[vmem] * 4,
        scratch_shapes=[
            block, block, block, block,
            pltpu.VMEM((2, 2, rows, width), jnp.bfloat16),
            pltpu.VMEM((2, 2, rows, width), jnp.bfloat16),
            pltpu.VMEM((2, 2, rows, width), jnp.bfloat16),
            pltpu.VMEM((2, rows, width), jnp.float32),
            pltpu.VMEM(doc_mask.shape, jnp.float32),
            pltpu.VMEM((rows, HEAD_DIM), jnp.float32),
            pltpu.SemaphoreType.DMA((4,)),
            pltpu.SemaphoreType.DMA((4 * GROUPS,)),
            pltpu.SemaphoreType.DMA((4 * GROUPS,)),
            pltpu.SemaphoreType.DMA((4 * GROUPS,)),
            pltpu.SemaphoreType.DMA((4 * GROUPS,)),
        ],
        compiler_params=pltpu.CompilerParams(
            collective_id=0, has_side_effects=True, vmem_limit_bytes=40 * 2**20
        ),
        cost_estimate=pl.CostEstimate(
            flops=12 * HEADS * rows * 3 * rows * HEAD_DIM,
            bytes_accessed=16 * rows * width,
            transcendentals=HEADS * rows * 3 * rows,
        ),
    )(queries, keys, values, out_grad, doc_mask, ratio_bins.reshape(1, rows))


def solution(mesh):
    split = P(("dp", "fsdp"), None)
    return jax.shard_map(
        local,
        mesh=mesh,
        in_specs=(split, split, split, split, P(("dp", "fsdp")), split),
        out_specs=(split, split, split, split),
        check_vma=False,
    )
```

```python
import functools
import math

import jax
import jax.numpy as jnp
from jax import lax
from jax.experimental import pallas as pl
from jax.experimental.pallas import tpu as pltpu
from jax.sharding import PartitionSpec as P

HEADS = 16
HEAD_DIM = 128
NBINS = 8
GROUP = 2
GROUPS = HEADS // GROUP
COLS = GROUP * HEAD_DIM
MASKED = -1e30
PIECES = 4
MESH = pl.DeviceIdType.MESH


def neighbour(step):
    dps, fsdps = lax.axis_size("dp"), lax.axis_size("fsdp")
    flat = lax.axis_index("dp") * fsdps + lax.axis_index("fsdp")
    flat = lax.rem(flat + step + dps * fsdps, dps * fsdps)
    return (flat // fsdps, lax.rem(flat, fsdps))


def dot(a, b, dims):
    return lax.dot_general(a, b, (dims, ((), ())), preferred_element_type=jnp.float32)


def kernel(
    queries, keys, values, out_grad, mask, bins,
    attended_hbm, query_grad_hbm, key_grad_hbm, value_grad_hbm,
    attended, query_grad, key_grad, value_grad, q_v, k_v, v_v, g_v, mask_v, bins_v, halo, sent, got, own, bias, weight,
    load_sem, out_sem, halo_send, halo_recv, term_send, term_recv,
):
    scale = 1.0 / math.sqrt(HEAD_DIM)
    rows = q_v.shape[0]
    sides = (neighbour(-1), neighbour(1))

    def load(at, src, dst):
        return pltpu.make_async_copy(src, dst, load_sem.at[at])

    loads = [
        load(0, keys, k_v),
        load(1, values, v_v),
        load(2, queries, q_v),
        load(3, out_grad, g_v),
        load(4, mask, mask_v),
        load(5, bins, bins_v),
    ]
    for copy in loads:
        copy.start()

    barrier = pltpu.get_barrier_semaphore()
    for side in sides:
        pl.semaphore_signal(barrier, inc=1, device_id=side, device_id_type=MESH)
    for copy in loads[:2]:
        copy.wait()
    pl.semaphore_wait(barrier, 2)

    def columns(group):
        return pl.ds(pl.multiple_of(group * COLS, COLS), COLS)

    def halo_copy(group, kind, side):
        src = (k_v, v_v)[kind]
        at = (kind * 2 + 1 - side) * GROUPS + group
        return pltpu.make_async_remote_copy(
            src_ref=src.at[:, columns(group)],
            dst_ref=halo.at[kind, 1 - side, :, columns(group)],
            send_sem=halo_send.at[at],
            recv_sem=halo_recv.at[at],
            device_id=sides[side],
            device_id_type=MESH,
        )

    def term_copy(group, kind, side):
        at = (kind * 2 + 1 - side) * GROUPS + group
        return pltpu.make_async_remote_copy(
            src_ref=sent.at[kind, side, :, columns(group)],
            dst_ref=got.at[kind, 1 - side, :, columns(group)],
            send_sem=term_send.at[at],
            recv_sem=term_recv.at[at],
            device_id=sides[side],
            device_id_type=MESH,
        )

    def out_copy(group, at):
        src = (attended, query_grad, key_grad, value_grad)[at]
        dst = (attended_hbm, query_grad_hbm, key_grad_hbm, value_grad_hbm)[at]
        here = columns(group)
        return pltpu.make_async_copy(
            src.at[:, here], dst.at[:, here], out_sem.at[at * GROUPS + group]
        )

    each = [(kind, side) for kind in range(2) for side in range(2)]

    def send_halo(group, carry):
        for kind, side in each:
            halo_copy(group, kind, side).start()
        return carry

    lax.fori_loop(0, GROUPS, send_halo, 0)

    for copy in loads[2:]:
        copy.wait()
    bias[...] = jnp.where(mask_v[...] == 1, 0.0, MASKED)
    ratio = NBINS / (bins_v[...].astype(jnp.float32) + 1.0)
    weight[...] = jnp.broadcast_to(ratio, (HEAD_DIM, rows)).T

    def attend(group, carry):
        for kind, side in each:
            halo_copy(group, kind, side).wait_recv()
        for head in range(GROUP):
            here = pl.ds(
                pl.multiple_of(group * COLS + head * HEAD_DIM, HEAD_DIM), HEAD_DIM
            )
            q = q_v[:, here]
            g = (g_v[:, here].astype(jnp.float32) * weight[...]).astype(jnp.bfloat16)
            k = jnp.concatenate([halo[0, 0, :, here], k_v[:, here], halo[0, 1, :, here]], axis=0)
            v = jnp.concatenate([halo[1, 0, :, here], v_v[:, here], halo[1, 1, :, here]], axis=0)
            allowed = bias[...] == 0.0
            scores = jnp.where(allowed, dot(q, k, ((1,), (1,))) * scale, MASKED)
            largest = jnp.max(scores, axis=1, keepdims=True)
            powers = jnp.exp(scores - largest)
            prob = powers / jnp.sum(powers, axis=1, keepdims=True)
            prob_w = prob.astype(jnp.bfloat16)
            out = dot(prob_w, v, ((1,), (0,))).astype(jnp.bfloat16)
            attended[:, here] = out
            delta = jnp.sum(
                g.astype(jnp.float32) * out.astype(jnp.float32), axis=1, keepdims=True
            )
            dprob = dot(g, v, ((1,), (1,)))
            dscore = (prob * (dprob - delta)).astype(jnp.bfloat16)
            query_grad[:, here] = (dot(dscore, k, ((1,), (0,))) * scale).astype(jnp.bfloat16)
            dk = dot(dscore, q, ((0,), (0,))) * scale
            dv = dot(prob_w, g, ((0,), (0,)))
            for kind, term in ((0, dk), (1, dv)):
                sent[kind, 0, :, here] = term[:rows].astype(jnp.bfloat16)
                own[kind, :, here] = term[rows : 2 * rows]
                sent[kind, 1, :, here] = term[2 * rows :].astype(jnp.bfloat16)
        for kind, side in each:
            term_copy(group, kind, side).start()
        out_copy(group, 0).start()
        out_copy(group, 1).start()
        return carry

    lax.fori_loop(0, GROUPS, attend, 0)

    def finish(group, carry):
        for kind, side in each:
            term_copy(group, kind, side).wait_recv()
        for kind, grad in ((0, key_grad), (1, value_grad)):
            here = columns(group)
            total = own[kind, :, here] + got[kind, 0, :, here].astype(jnp.float32)
            grad[:, here] = (total + got[kind, 1, :, here].astype(jnp.float32)).astype(jnp.bfloat16)
            out_copy(group, 2 + kind).start()
        return carry

    lax.fori_loop(0, GROUPS, finish, 0)

    def drain(group, carry):
        for kind, side in each:
            halo_copy(group, kind, side).wait_send()
            term_copy(group, kind, side).wait_send()
        for at in range(4):
            out_copy(group, at).wait()
        return carry

    lax.fori_loop(0, GROUPS, drain, 0)


def hand_on(*refs):
    sources, results, held, in_sem, out_sem = refs[:4], refs[4:8], *refs[8:]
    rows = sources[0].shape[0] // PIECES
    ins, outs = [], []
    for at in range(4):
        for piece in range(PIECES):
            here, sem = pl.ds(piece * rows, rows), at * PIECES + piece
            held_here = held.at[at, here]
            ins.append(pltpu.make_async_copy(sources[at].at[here], held_here, in_sem.at[sem]))
            outs.append(pltpu.make_async_copy(held_here, results[at].at[here], out_sem.at[sem]))
    for copy in ins:
        copy.start()
    for arrived, onward in zip(ins, outs):
        arrived.wait()
        onward.start()
    for copy in outs:
        copy.wait()


def local(queries, keys, values, doc_mask, ratio_bins, out_grad):
    rows, width = queries.shape
    result = jax.ShapeDtypeStruct((rows, width), jnp.bfloat16)
    hbm = pl.BlockSpec(memory_space=pltpu.HBM)
    block = pltpu.VMEM((rows, width), jnp.bfloat16)
    inner = pl.pallas_call(
        kernel,
        out_shape=[result] * 4,
        in_specs=[hbm] * 6,
        out_specs=[hbm] * 4,
        scratch_shapes=[
            block, block, block, block, block, block, block, block,
            pltpu.VMEM(doc_mask.shape, doc_mask.dtype),
            pltpu.VMEM((1, rows), ratio_bins.dtype),
            pltpu.VMEM((2, 2, rows, width), jnp.bfloat16),
            pltpu.VMEM((2, 2, rows, width), jnp.bfloat16),
            pltpu.VMEM((2, 2, rows, width), jnp.bfloat16),
            pltpu.VMEM((2, rows, width), jnp.float32),
            pltpu.VMEM(doc_mask.shape, jnp.float32),
            pltpu.VMEM((rows, HEAD_DIM), jnp.float32),
            pltpu.SemaphoreType.DMA((6,)),
            pltpu.SemaphoreType.DMA((4 * GROUPS,)),
            pltpu.SemaphoreType.DMA((4 * GROUPS,)),
            pltpu.SemaphoreType.DMA((4 * GROUPS,)),
            pltpu.SemaphoreType.DMA((4 * GROUPS,)),
            pltpu.SemaphoreType.DMA((4 * GROUPS,)),
        ],
        compiler_params=pltpu.CompilerParams(
            collective_id=0, has_side_effects=True, vmem_limit_bytes=60 * 2**20
        ),
        cost_estimate=pl.CostEstimate(
            flops=12 * HEADS * rows * 3 * rows * HEAD_DIM,
            bytes_accessed=16 * rows * width,
            transcendentals=HEADS * rows * 3 * rows,
        ),
    )(queries, keys, values, out_grad, doc_mask, ratio_bins.reshape(1, rows))
    return pl.pallas_call(
        hand_on,
        out_shape=[result] * 4,
        in_specs=[hbm] * 4,
        out_specs=[hbm] * 4,
        scratch_shapes=[
            pltpu.VMEM((4, rows, width), jnp.bfloat16),
            pltpu.SemaphoreType.DMA((4 * PIECES,)),
            pltpu.SemaphoreType.DMA((4 * PIECES,)),
        ],
        compiler_params=pltpu.CompilerParams(vmem_limit_bytes=60 * 2**20),
    )(*inner)


def solution(mesh):
    split = P(("dp", "fsdp"), None)
    return jax.shard_map(
        local,
        mesh=mesh,
        in_specs=(split, split, split, split, P(("dp", "fsdp")), split),
        out_specs=(split, split, split, split),
        check_vma=False,
    )
```

```python
import functools
import math

import jax
import jax.numpy as jnp
from jax import lax
from jax.experimental import pallas as pl
from jax.experimental.pallas import tpu as pltpu
from jax.sharding import PartitionSpec as P

HEADS = 16
HEAD_DIM = 128
NBINS = 8
GROUP = 2
GROUPS = HEADS // GROUP
COLS = GROUP * HEAD_DIM
MASKED = -1e30
PIECES = 4
MESH = pl.DeviceIdType.MESH


def neighbour(step):
    dps, fsdps = lax.axis_size("dp"), lax.axis_size("fsdp")
    flat = lax.axis_index("dp") * fsdps + lax.axis_index("fsdp")
    flat = lax.rem(flat + step + dps * fsdps, dps * fsdps)
    return (flat // fsdps, lax.rem(flat, fsdps))


def dot(a, b, dims):
    return lax.dot_general(a, b, (dims, ((), ())), preferred_element_type=jnp.float32)


def kernel(
    queries, keys, values, out_grad, mask, bins,
    attended_hbm, query_grad_hbm, key_grad_hbm, value_grad_hbm,
    attended, query_grad, key_grad, value_grad, q_v, k_v, v_v, g_v, mask_v, bins_v, halo, sent, got, own, bias, weight,
    ready, load_sem, out_sem, halo_send, halo_recv, term_send, term_recv,
):
    scale = 1.0 / math.sqrt(HEAD_DIM)
    rows = q_v.shape[0]
    sides = (neighbour(-1), neighbour(1))

    def load(at, src, dst):
        return pltpu.make_async_copy(src, dst, load_sem.at[at])

    loads = [
        load(0, keys, k_v),
        load(1, values, v_v),
        load(2, queries, q_v),
        load(3, out_grad, g_v),
        load(4, mask, mask_v),
        load(5, bins, bins_v),
    ]
    for copy in loads:
        copy.start()

    barrier = pltpu.get_barrier_semaphore()
    pl.semaphore_signal(barrier, inc=1, device_id=sides[0], device_id_type=MESH)
    for copy in loads[:2]:
        copy.wait()
    pl.semaphore_wait(barrier, 1)
    pl.semaphore_signal(ready, inc=1, device_id=sides[1], device_id_type=MESH)

    def columns(group):
        return pl.ds(pl.multiple_of(group * COLS, COLS), COLS)

    def halo_copy(group, kind, side):
        src = (k_v, v_v)[kind]
        at = (kind * 2 + 1 - side) * GROUPS + group
        return pltpu.make_async_remote_copy(
            src_ref=src.at[:, columns(group)],
            dst_ref=halo.at[kind, 1 - side, :, columns(group)],
            send_sem=halo_send.at[at],
            recv_sem=halo_recv.at[at],
            device_id=sides[side],
            device_id_type=MESH,
        )

    def term_copy(group, kind, side):
        at = (kind * 2 + 1 - side) * GROUPS + group
        return pltpu.make_async_remote_copy(
            src_ref=sent.at[kind, side, :, columns(group)],
            dst_ref=got.at[kind, 1 - side, :, columns(group)],
            send_sem=term_send.at[at],
            recv_sem=term_recv.at[at],
            device_id=sides[side],
            device_id_type=MESH,
        )

    def out_copy(group, at):
        src = (attended, query_grad, key_grad, value_grad)[at]
        dst = (attended_hbm, query_grad_hbm, key_grad_hbm, value_grad_hbm)[at]
        here = columns(group)
        return pltpu.make_async_copy(
            src.at[:, here], dst.at[:, here], out_sem.at[at * GROUPS + group]
        )

    each = [(kind, side) for kind in range(2) for side in range(2)]

    def send_halo(side, group, carry):
        for kind in range(2):
            halo_copy(group, kind, side).start()
        return carry

    lax.fori_loop(0, GROUPS, functools.partial(send_halo, 1), 0)
    pl.semaphore_wait(ready, 1)
    lax.fori_loop(0, GROUPS, functools.partial(send_halo, 0), 0)

    for copy in loads[2:]:
        copy.wait()
    bias[...] = jnp.where(mask_v[...] == 1, 0.0, MASKED)
    ratio = NBINS / (bins_v[...].astype(jnp.float32) + 1.0)
    weight[...] = jnp.broadcast_to(ratio, (HEAD_DIM, rows)).T

    def attend(group, carry):
        for kind, side in each:
            halo_copy(group, kind, side).wait_recv()
        for head in range(GROUP):
            here = pl.ds(
                pl.multiple_of(group * COLS + head * HEAD_DIM, HEAD_DIM), HEAD_DIM
            )
            q = q_v[:, here]
            g = (g_v[:, here].astype(jnp.float32) * weight[...]).astype(jnp.bfloat16)
            k = jnp.concatenate([halo[0, 0, :, here], k_v[:, here], halo[0, 1, :, here]], axis=0)
            v = jnp.concatenate([halo[1, 0, :, here], v_v[:, here], halo[1, 1, :, here]], axis=0)
            allowed = bias[...] == 0.0
            scores = jnp.where(allowed, dot(q, k, ((1,), (1,))) * scale, MASKED)
            largest = jnp.max(scores, axis=1, keepdims=True)
            powers = jnp.exp(scores - largest)
            prob = powers / jnp.sum(powers, axis=1, keepdims=True)
            prob_w = prob.astype(jnp.bfloat16)
            out = dot(prob_w, v, ((1,), (0,))).astype(jnp.bfloat16)
            attended[:, here] = out
            delta = jnp.sum(
                g.astype(jnp.float32) * out.astype(jnp.float32), axis=1, keepdims=True
            )
            dprob = dot(g, v, ((1,), (1,)))
            dscore = (prob * (dprob - delta)).astype(jnp.bfloat16)
            query_grad[:, here] = (dot(dscore, k, ((1,), (0,))) * scale).astype(jnp.bfloat16)
            dk = dot(dscore, q, ((0,), (0,))) * scale
            dv = dot(prob_w, g, ((0,), (0,)))
            for kind, term in ((0, dk), (1, dv)):
                sent[kind, 0, :, here] = term[:rows].astype(jnp.bfloat16)
                own[kind, :, here] = term[rows : 2 * rows]
                sent[kind, 1, :, here] = term[2 * rows :].astype(jnp.bfloat16)
        for kind, side in each:
            term_copy(group, kind, side).start()
        out_copy(group, 0).start()
        out_copy(group, 1).start()
        return carry

    lax.fori_loop(0, GROUPS, attend, 0)

    def finish(group, carry):
        for kind, side in each:
            term_copy(group, kind, side).wait_recv()
        for kind, grad in ((0, key_grad), (1, value_grad)):
            here = columns(group)
            total = own[kind, :, here] + got[kind, 0, :, here].astype(jnp.float32)
            grad[:, here] = (total + got[kind, 1, :, here].astype(jnp.float32)).astype(jnp.bfloat16)
            out_copy(group, 2 + kind).start()
        return carry

    lax.fori_loop(0, GROUPS, finish, 0)

    def drain(group, carry):
        for kind, side in each:
            halo_copy(group, kind, side).wait_send()
            term_copy(group, kind, side).wait_send()
        for at in range(4):
            out_copy(group, at).wait()
        return carry

    lax.fori_loop(0, GROUPS, drain, 0)


def hand_on(*refs):
    sources, results, held, in_sem, out_sem = refs[:4], refs[4:8], *refs[8:]
    rows = sources[0].shape[0] // PIECES
    ins, outs = [], []
    for at in range(4):
        for piece in range(PIECES):
            here, sem = pl.ds(piece * rows, rows), at * PIECES + piece
            held_here = held.at[at, here]
            ins.append(pltpu.make_async_copy(sources[at].at[here], held_here, in_sem.at[sem]))
            outs.append(pltpu.make_async_copy(held_here, results[at].at[here], out_sem.at[sem]))
    for copy in ins:
        copy.start()
    for arrived, onward in zip(ins, outs):
        arrived.wait()
        onward.start()
    for copy in outs:
        copy.wait()


def local(queries, keys, values, doc_mask, ratio_bins, out_grad):
    rows, width = queries.shape
    result = jax.ShapeDtypeStruct((rows, width), jnp.bfloat16)
    hbm = pl.BlockSpec(memory_space=pltpu.HBM)
    block = pltpu.VMEM((rows, width), jnp.bfloat16)
    inner = pl.pallas_call(
        kernel,
        out_shape=[result] * 4,
        in_specs=[hbm] * 6,
        out_specs=[hbm] * 4,
        scratch_shapes=[
            block, block, block, block, block, block, block, block,
            pltpu.VMEM(doc_mask.shape, doc_mask.dtype),
            pltpu.VMEM((1, rows), ratio_bins.dtype),
            pltpu.VMEM((2, 2, rows, width), jnp.bfloat16),
            pltpu.VMEM((2, 2, rows, width), jnp.bfloat16),
            pltpu.VMEM((2, 2, rows, width), jnp.bfloat16),
            pltpu.VMEM((2, rows, width), jnp.float32),
            pltpu.VMEM(doc_mask.shape, jnp.float32),
            pltpu.VMEM((rows, HEAD_DIM), jnp.float32),
            pltpu.SemaphoreType.REGULAR,
            pltpu.SemaphoreType.DMA((6,)),
            pltpu.SemaphoreType.DMA((4 * GROUPS,)),
            pltpu.SemaphoreType.DMA((4 * GROUPS,)),
            pltpu.SemaphoreType.DMA((4 * GROUPS,)),
            pltpu.SemaphoreType.DMA((4 * GROUPS,)),
            pltpu.SemaphoreType.DMA((4 * GROUPS,)),
        ],
        compiler_params=pltpu.CompilerParams(
            collective_id=0, has_side_effects=True, vmem_limit_bytes=60 * 2**20
        ),
        cost_estimate=pl.CostEstimate(
            flops=12 * HEADS * rows * 3 * rows * HEAD_DIM,
            bytes_accessed=16 * rows * width,
            transcendentals=HEADS * rows * 3 * rows,
        ),
    )(queries, keys, values, out_grad, doc_mask, ratio_bins.reshape(1, rows))
    return pl.pallas_call(
        hand_on,
        out_shape=[result] * 4,
        in_specs=[hbm] * 4,
        out_specs=[hbm] * 4,
        scratch_shapes=[
            pltpu.VMEM((4, rows, width), jnp.bfloat16),
            pltpu.SemaphoreType.DMA((4 * PIECES,)),
            pltpu.SemaphoreType.DMA((4 * PIECES,)),
        ],
        compiler_params=pltpu.CompilerParams(vmem_limit_bytes=60 * 2**20),
    )(*inner)


def solution(mesh):
    split = P(("dp", "fsdp"), None)
    return jax.shard_map(
        local,
        mesh=mesh,
        in_specs=(split, split, split, split, P(("dp", "fsdp")), split),
        out_specs=(split, split, split, split),
        check_vma=False,
    )
```

```python
import functools
import math

import jax
import jax.numpy as jnp
from jax import lax
from jax.experimental import pallas as pl
from jax.experimental.pallas import tpu as pltpu
from jax.sharding import PartitionSpec as P

HEADS = 16
HEAD_DIM = 128
NBINS = 8
GROUP = 4
GROUPS = HEADS // GROUP
COLS = GROUP * HEAD_DIM
MASKED = -1e30
PIECES = 2
MESH = pl.DeviceIdType.MESH


def neighbour(step):
    dps, fsdps = lax.axis_size("dp"), lax.axis_size("fsdp")
    flat = lax.axis_index("dp") * fsdps + lax.axis_index("fsdp")
    flat = lax.rem(flat + step + dps * fsdps, dps * fsdps)
    return (flat // fsdps, lax.rem(flat, fsdps))


def dot(a, b, dims):
    return lax.dot_general(a, b, (dims, ((), ())), preferred_element_type=jnp.float32)


def kernel(
    queries, keys, values, out_grad, mask, bins,
    attended_hbm, query_grad_hbm, key_grad_hbm, value_grad_hbm,
    attended, query_grad, key_grad, value_grad, q_v, k_v, v_v, g_v, mask_v, bins_v, halo, sent, got, own, bias, weight,
    ready, load_sem, out_sem, halo_send, halo_recv, term_send, term_recv,
):
    scale = 1.0 / math.sqrt(HEAD_DIM)
    rows = q_v.shape[0]
    sides = (neighbour(-1), neighbour(1))

    def load(at, src, dst):
        return pltpu.make_async_copy(src, dst, load_sem.at[at])

    loads = [
        load(0, keys, k_v),
        load(1, values, v_v),
        load(2, queries, q_v),
        load(3, out_grad, g_v),
        load(4, mask, mask_v),
        load(5, bins, bins_v),
    ]
    for copy in loads:
        copy.start()

    barrier = pltpu.get_barrier_semaphore()
    pl.semaphore_signal(barrier, inc=1, device_id=sides[0], device_id_type=MESH)
    for copy in loads[:2]:
        copy.wait()
    pl.semaphore_wait(barrier, 1)
    pl.semaphore_signal(ready, inc=1, device_id=sides[1], device_id_type=MESH)

    def columns(group):
        return pl.ds(pl.multiple_of(group * COLS, COLS), COLS)

    def halo_copy(group, kind, side):
        src = (k_v, v_v)[kind]
        at = (kind * 2 + 1 - side) * GROUPS + group
        return pltpu.make_async_remote_copy(
            src_ref=src.at[:, columns(group)],
            dst_ref=halo.at[kind, 1 - side, :, columns(group)],
            send_sem=halo_send.at[at],
            recv_sem=halo_recv.at[at],
            device_id=sides[side],
            device_id_type=MESH,
        )

    def term_copy(group, kind, side):
        at = (kind * 2 + 1 - side) * GROUPS + group
        return pltpu.make_async_remote_copy(
            src_ref=sent.at[kind, side, :, columns(group)],
            dst_ref=got.at[kind, 1 - side, :, columns(group)],
            send_sem=term_send.at[at],
            recv_sem=term_recv.at[at],
            device_id=sides[side],
            device_id_type=MESH,
        )

    def out_copy(group, at):
        src = (attended, query_grad, key_grad, value_grad)[at]
        dst = (attended_hbm, query_grad_hbm, key_grad_hbm, value_grad_hbm)[at]
        here = columns(group)
        return pltpu.make_async_copy(
            src.at[:, here], dst.at[:, here], out_sem.at[at * GROUPS + group]
        )

    each = [(kind, side) for kind in range(2) for side in range(2)]

    def send_halo(side, group, carry):
        for kind in range(2):
            halo_copy(group, kind, side).start()
        return carry

    lax.fori_loop(0, GROUPS, functools.partial(send_halo, 1), 0)
    pl.semaphore_wait(ready, 1)
    lax.fori_loop(0, GROUPS, functools.partial(send_halo, 0), 0)

    for copy in loads[2:]:
        copy.wait()
    bias[...] = jnp.where(mask_v[...] == 1, 0.0, MASKED)
    ratio = NBINS / (bins_v[...].astype(jnp.float32) + 1.0)
    weight[...] = jnp.broadcast_to(ratio, (HEAD_DIM, rows)).T

    def attend(group, carry):
        for kind, side in each:
            halo_copy(group, kind, side).wait_recv()
        for head in range(GROUP):
            here = pl.ds(
                pl.multiple_of(group * COLS + head * HEAD_DIM, HEAD_DIM), HEAD_DIM
            )
            q = q_v[:, here]
            g = (g_v[:, here].astype(jnp.float32) * weight[...]).astype(jnp.bfloat16)
            k = jnp.concatenate([halo[0, 0, :, here], k_v[:, here], halo[0, 1, :, here]], axis=0)
            v = jnp.concatenate([halo[1, 0, :, here], v_v[:, here], halo[1, 1, :, here]], axis=0)
            allowed = bias[...] == 0.0
            scores = jnp.where(allowed, dot(q, k, ((1,), (1,))) * scale, MASKED)
            largest = jnp.max(scores, axis=1, keepdims=True)
            powers = jnp.exp(scores - largest)
            prob = powers / jnp.sum(powers, axis=1, keepdims=True)
            prob_w = prob.astype(jnp.bfloat16)
            out = dot(prob_w, v, ((1,), (0,))).astype(jnp.bfloat16)
            attended[:, here] = out
            delta = jnp.sum(
                g.astype(jnp.float32) * out.astype(jnp.float32), axis=1, keepdims=True
            )
            dprob = dot(g, v, ((1,), (1,)))
            dscore = (prob * (dprob - delta)).astype(jnp.bfloat16)
            query_grad[:, here] = (dot(dscore, k, ((1,), (0,))) * scale).astype(jnp.bfloat16)
            dk = dot(dscore, q, ((0,), (0,))) * scale
            dv = dot(prob_w, g, ((0,), (0,)))
            for kind, term in ((0, dk), (1, dv)):
                sent[kind, 0, :, here] = term[:rows].astype(jnp.bfloat16)
                own[kind, :, here] = term[rows : 2 * rows]
                sent[kind, 1, :, here] = term[2 * rows :].astype(jnp.bfloat16)
        for kind, side in each:
            term_copy(group, kind, side).start()
        out_copy(group, 0).start()
        out_copy(group, 1).start()
        return carry

    lax.fori_loop(0, GROUPS, attend, 0)

    def drain(group, carry):
        for kind, side in each:
            halo_copy(group, kind, side).wait_send()
        for at in range(2):
            out_copy(group, at).wait()
        return carry

    lax.fori_loop(0, GROUPS, drain, 0)

    def settle(group):
        for kind, side in each:
            term_copy(group, kind, side).wait_send()
        for at in range(2, 4):
            out_copy(group, at).wait()

    def finish(group, carry):
        for kind, side in each:
            term_copy(group, kind, side).wait_recv()
        for kind, grad in ((0, key_grad), (1, value_grad)):
            here = columns(group)
            total = own[kind, :, here] + got[kind, 0, :, here].astype(jnp.float32)
            grad[:, here] = (total + got[kind, 1, :, here].astype(jnp.float32)).astype(jnp.bfloat16)
            out_copy(group, 2 + kind).start()

        @pl.when(group > 0)
        def _():
            settle(group - 1)

        return carry

    lax.fori_loop(0, GROUPS, finish, 0)
    settle(GROUPS - 1)


def hand_on(*refs):
    sources, results, held, in_sem, out_sem = refs[:4], refs[4:8], *refs[8:]
    rows = sources[0].shape[0] // PIECES
    ins, outs = [], []
    for at in range(4):
        for piece in range(PIECES):
            here, sem = pl.ds(piece * rows, rows), at * PIECES + piece
            held_here = held.at[at, here]
            ins.append(pltpu.make_async_copy(sources[at].at[here], held_here, in_sem.at[sem]))
            outs.append(pltpu.make_async_copy(held_here, results[at].at[here], out_sem.at[sem]))
    for copy in ins:
        copy.start()
    for arrived, onward in zip(ins, outs):
        arrived.wait()
        onward.start()
    for copy in outs:
        copy.wait()


def local(queries, keys, values, doc_mask, ratio_bins, out_grad):
    rows, width = queries.shape
    result = jax.ShapeDtypeStruct((rows, width), jnp.bfloat16)
    hbm = pl.BlockSpec(memory_space=pltpu.HBM)
    block = pltpu.VMEM((rows, width), jnp.bfloat16)
    inner = pl.pallas_call(
        kernel,
        out_shape=[result] * 4,
        in_specs=[hbm] * 6,
        out_specs=[hbm] * 4,
        scratch_shapes=[
            block, block, block, block, block, block, block, block,
            pltpu.VMEM(doc_mask.shape, doc_mask.dtype),
            pltpu.VMEM((1, rows), ratio_bins.dtype),
            pltpu.VMEM((2, 2, rows, width), jnp.bfloat16),
            pltpu.VMEM((2, 2, rows, width), jnp.bfloat16),
            pltpu.VMEM((2, 2, rows, width), jnp.bfloat16),
            pltpu.VMEM((2, rows, width), jnp.float32),
            pltpu.VMEM(doc_mask.shape, jnp.float32),
            pltpu.VMEM((rows, HEAD_DIM), jnp.float32),
            pltpu.SemaphoreType.REGULAR,
            pltpu.SemaphoreType.DMA((6,)),
            pltpu.SemaphoreType.DMA((4 * GROUPS,)),
            pltpu.SemaphoreType.DMA((4 * GROUPS,)),
            pltpu.SemaphoreType.DMA((4 * GROUPS,)),
            pltpu.SemaphoreType.DMA((4 * GROUPS,)),
            pltpu.SemaphoreType.DMA((4 * GROUPS,)),
        ],
        compiler_params=pltpu.CompilerParams(
            collective_id=0, has_side_effects=True, vmem_limit_bytes=60 * 2**20
        ),
        cost_estimate=pl.CostEstimate(
            flops=12 * HEADS * rows * 3 * rows * HEAD_DIM,
            bytes_accessed=16 * rows * width,
            transcendentals=HEADS * rows * 3 * rows,
        ),
    )(queries, keys, values, out_grad, doc_mask, ratio_bins.reshape(1, rows))
    return pl.pallas_call(
        hand_on,
        out_shape=[result] * 4,
        in_specs=[hbm] * 4,
        out_specs=[hbm] * 4,
        scratch_shapes=[
            pltpu.VMEM((4, rows, width), jnp.bfloat16),
            pltpu.SemaphoreType.DMA((4 * PIECES,)),
            pltpu.SemaphoreType.DMA((4 * PIECES,)),
        ],
        compiler_params=pltpu.CompilerParams(vmem_limit_bytes=60 * 2**20),
    )(*inner)


def solution(mesh):
    split = P(("dp", "fsdp"), None)
    return jax.shard_map(
        local,
        mesh=mesh,
        in_specs=(split, split, split, split, P(("dp", "fsdp")), split),
        out_specs=(split, split, split, split),
        check_vma=False,
    )
```

```python
import functools
import math

import jax
import jax.numpy as jnp
from jax import lax
from jax.experimental import pallas as pl
from jax.experimental.pallas import tpu as pltpu
from jax.sharding import PartitionSpec as P

HEADS = 16
HEAD_DIM = 128
NBINS = 8
GROUP = 8
GROUPS = HEADS // GROUP
COLS = GROUP * HEAD_DIM
MASKED = -1e30
PIECES = 2
MESH = pl.DeviceIdType.MESH


def neighbour(step):
    dps, fsdps = lax.axis_size("dp"), lax.axis_size("fsdp")
    flat = lax.axis_index("dp") * fsdps + lax.axis_index("fsdp")
    flat = lax.rem(flat + step + dps * fsdps, dps * fsdps)
    return (flat // fsdps, lax.rem(flat, fsdps))


def dot(a, b, dims):
    return lax.dot_general(a, b, (dims, ((), ())), preferred_element_type=jnp.float32)


def kernel(
    queries, keys, values, out_grad, mask, bins,
    attended_hbm, query_grad_hbm, key_grad_hbm, value_grad_hbm,
    attended, query_grad, key_grad, value_grad, q_v, k_v, v_v, g_v, mask_v, bins_v, halo, sent, got, own, bias, weight,
    ready, load_sem, out_sem, halo_send, halo_recv, term_send, term_recv,
):
    scale = 1.0 / math.sqrt(HEAD_DIM)
    rows = q_v.shape[0]
    sides = (neighbour(-1), neighbour(1))

    def load(at, src, dst):
        return pltpu.make_async_copy(src, dst, load_sem.at[at])

    loads = [
        load(0, keys, k_v),
        load(1, values, v_v),
        load(2, queries, q_v),
        load(3, out_grad, g_v),
        load(4, mask, mask_v),
        load(5, bins, bins_v),
    ]
    for copy in loads:
        copy.start()

    barrier = pltpu.get_barrier_semaphore()
    pl.semaphore_signal(barrier, inc=1, device_id=sides[0], device_id_type=MESH)
    for copy in loads[:2]:
        copy.wait()
    pl.semaphore_wait(barrier, 1)
    pl.semaphore_signal(ready, inc=1, device_id=sides[1], device_id_type=MESH)

    def columns(group):
        return pl.ds(pl.multiple_of(group * COLS, COLS), COLS)

    def halo_copy(group, kind, side):
        src = (k_v, v_v)[kind]
        at = (kind * 2 + 1 - side) * GROUPS + group
        return pltpu.make_async_remote_copy(
            src_ref=src.at[:, columns(group)],
            dst_ref=halo.at[kind, 1 - side, :, columns(group)],
            send_sem=halo_send.at[at],
            recv_sem=halo_recv.at[at],
            device_id=sides[side],
            device_id_type=MESH,
        )

    def term_copy(group, kind, side):
        at = (kind * 2 + 1 - side) * GROUPS + group
        return pltpu.make_async_remote_copy(
            src_ref=sent.at[kind, side, :, columns(group)],
            dst_ref=got.at[kind, 1 - side, :, columns(group)],
            send_sem=term_send.at[at],
            recv_sem=term_recv.at[at],
            device_id=sides[side],
            device_id_type=MESH,
        )

    def out_copy(group, at):
        src = (attended, query_grad, key_grad, value_grad)[at]
        dst = (attended_hbm, query_grad_hbm, key_grad_hbm, value_grad_hbm)[at]
        here = columns(group)
        return pltpu.make_async_copy(
            src.at[:, here], dst.at[:, here], out_sem.at[at * GROUPS + group]
        )

    each = [(kind, side) for kind in range(2) for side in range(2)]

    def send_halo(side, group, carry):
        for kind in range(2):
            halo_copy(group, kind, side).start()
        return carry

    lax.fori_loop(0, GROUPS, functools.partial(send_halo, 1), 0)
    pl.semaphore_wait(ready, 1)
    lax.fori_loop(0, GROUPS, functools.partial(send_halo, 0), 0)

    for copy in loads[2:]:
        copy.wait()
    bias[...] = jnp.where(mask_v[...] == 1, 0.0, MASKED)
    ratio = NBINS / (bins_v[...].astype(jnp.float32) + 1.0)
    weight[...] = jnp.broadcast_to(ratio, (HEAD_DIM, rows)).T

    def attend(group, carry):
        for kind, side in each:
            halo_copy(group, kind, side).wait_recv()
        for head in range(GROUP):
            here = pl.ds(
                pl.multiple_of(group * COLS + head * HEAD_DIM, HEAD_DIM), HEAD_DIM
            )
            q = q_v[:, here]
            g = (g_v[:, here].astype(jnp.float32) * weight[...]).astype(jnp.bfloat16)
            k = jnp.concatenate([halo[0, 0, :, here], k_v[:, here], halo[0, 1, :, here]], axis=0)
            v = jnp.concatenate([halo[1, 0, :, here], v_v[:, here], halo[1, 1, :, here]], axis=0)
            allowed = bias[...] == 0.0
            scores = jnp.where(allowed, dot(q, k, ((1,), (1,))) * scale, MASKED)
            largest = jnp.max(scores, axis=1, keepdims=True)
            powers = jnp.exp(scores - largest)
            prob = powers / jnp.sum(powers, axis=1, keepdims=True)
            prob_w = prob.astype(jnp.bfloat16)
            out = dot(prob_w, v, ((1,), (0,))).astype(jnp.bfloat16)
            attended[:, here] = out
            delta = jnp.sum(
                g.astype(jnp.float32) * out.astype(jnp.float32), axis=1, keepdims=True
            )
            dprob = dot(g, v, ((1,), (1,)))
            dscore = (prob * (dprob - delta)).astype(jnp.bfloat16)
            query_grad[:, here] = (dot(dscore, k, ((1,), (0,))) * scale).astype(jnp.bfloat16)
            dk = dot(dscore, q, ((0,), (0,))) * scale
            dv = dot(prob_w, g, ((0,), (0,)))
            for kind, term in ((0, dk), (1, dv)):
                sent[kind, 0, :, here] = term[:rows].astype(jnp.bfloat16)
                own[kind, :, here] = term[rows : 2 * rows]
                sent[kind, 1, :, here] = term[2 * rows :].astype(jnp.bfloat16)
        for kind, side in each:
            term_copy(group, kind, side).start()
        out_copy(group, 0).start()
        out_copy(group, 1).start()
        return carry

    lax.fori_loop(0, GROUPS, attend, 0)

    def drain(group, carry):
        for kind, side in each:
            halo_copy(group, kind, side).wait_send()
        for at in range(2):
            out_copy(group, at).wait()
        return carry

    lax.fori_loop(0, GROUPS, drain, 0)

    def settle(group):
        for kind, side in each:
            term_copy(group, kind, side).wait_send()
        for at in range(2, 4):
            out_copy(group, at).wait()

    def finish(group, carry):
        for kind, side in each:
            term_copy(group, kind, side).wait_recv()
        for kind, grad in ((0, key_grad), (1, value_grad)):
            here = columns(group)
            total = own[kind, :, here] + got[kind, 0, :, here].astype(jnp.float32)
            grad[:, here] = (total + got[kind, 1, :, here].astype(jnp.float32)).astype(jnp.bfloat16)
            out_copy(group, 2 + kind).start()

        @pl.when(group > 0)
        def _():
            settle(group - 1)

        return carry

    lax.fori_loop(0, GROUPS, finish, 0)
    settle(GROUPS - 1)


def hand_on(*refs):
    sources, results, held, in_sem, out_sem = refs[:4], refs[4:8], *refs[8:]
    rows = sources[0].shape[0] // PIECES
    ins, outs = [], []
    for at in range(4):
        for piece in range(PIECES):
            here, sem = pl.ds(piece * rows, rows), at * PIECES + piece
            held_here = held.at[at, here]
            ins.append(pltpu.make_async_copy(sources[at].at[here], held_here, in_sem.at[sem]))
            outs.append(pltpu.make_async_copy(held_here, results[at].at[here], out_sem.at[sem]))
    for copy in ins:
        copy.start()
    for arrived, onward in zip(ins, outs):
        arrived.wait()
        onward.start()
    for copy in outs:
        copy.wait()


def local(queries, keys, values, doc_mask, ratio_bins, out_grad):
    rows, width = queries.shape
    result = jax.ShapeDtypeStruct((rows, width), jnp.bfloat16)
    hbm = pl.BlockSpec(memory_space=pltpu.HBM)
    block = pltpu.VMEM((rows, width), jnp.bfloat16)
    inner = pl.pallas_call(
        kernel,
        out_shape=[result] * 4,
        in_specs=[hbm] * 6,
        out_specs=[hbm] * 4,
        scratch_shapes=[
            block, block, block, block, block, block, block, block,
            pltpu.VMEM(doc_mask.shape, doc_mask.dtype),
            pltpu.VMEM((1, rows), ratio_bins.dtype),
            pltpu.VMEM((2, 2, rows, width), jnp.bfloat16),
            pltpu.VMEM((2, 2, rows, width), jnp.bfloat16),
            pltpu.VMEM((2, 2, rows, width), jnp.bfloat16),
            pltpu.VMEM((2, rows, width), jnp.float32),
            pltpu.VMEM(doc_mask.shape, jnp.float32),
            pltpu.VMEM((rows, HEAD_DIM), jnp.float32),
            pltpu.SemaphoreType.REGULAR,
            pltpu.SemaphoreType.DMA((6,)),
            pltpu.SemaphoreType.DMA((4 * GROUPS,)),
            pltpu.SemaphoreType.DMA((4 * GROUPS,)),
            pltpu.SemaphoreType.DMA((4 * GROUPS,)),
            pltpu.SemaphoreType.DMA((4 * GROUPS,)),
            pltpu.SemaphoreType.DMA((4 * GROUPS,)),
        ],
        compiler_params=pltpu.CompilerParams(
            collective_id=0, has_side_effects=True, vmem_limit_bytes=60 * 2**20
        ),
        cost_estimate=pl.CostEstimate(
            flops=12 * HEADS * rows * 3 * rows * HEAD_DIM,
            bytes_accessed=16 * rows * width,
            transcendentals=HEADS * rows * 3 * rows,
        ),
    )(queries, keys, values, out_grad, doc_mask, ratio_bins.reshape(1, rows))
    return pl.pallas_call(
        hand_on,
        out_shape=[result] * 4,
        in_specs=[hbm] * 4,
        out_specs=[hbm] * 4,
        scratch_shapes=[
            pltpu.VMEM((4, rows, width), jnp.bfloat16),
            pltpu.SemaphoreType.DMA((4 * PIECES,)),
            pltpu.SemaphoreType.DMA((4 * PIECES,)),
        ],
        compiler_params=pltpu.CompilerParams(vmem_limit_bytes=60 * 2**20),
    )(*inner)


def solution(mesh):
    split = P(("dp", "fsdp"), None)
    return jax.shard_map(
        local,
        mesh=mesh,
        in_specs=(split, split, split, split, P(("dp", "fsdp")), split),
        out_specs=(split, split, split, split),
        check_vma=False,
    )
```
